32 devices in a mesh: surf: 8 (over z, x), rad: 4 (over y, core).
Axes of the slice: x: 2, y: 2, z: 4, core: 2. Of those that a mesh axis runs over, the one named last changes fastest.
Arguments:
- displacement: float32 [3, 128, 32, 512], P(None, 'surf', 'rad'), may hold values from -6 to 6
- velocity: float32 [3, 128, 32, 512], P(None, 'surf', 'rad'), may hold values from -6 to 6
- source: float32 [3, 128, 32, 512], P(None, 'surf', 'rad'), may hold values from -6 to 6
- lame_first: float32 [128, 32, 512], P('surf', 'rad'), may hold values from 0.5 to 2
- shear_modulus: float32 [128, 32, 512], P('surf', 'rad'), may hold values from 0.5 to 2
- density: float32 [128, 32, 512], P('surf', 'rad'), may hold values from 1 to 3
- shell_kappa: float32 [32, 4, 128], P('surf'), may hold values from 0.5 to 4
Outputs:
- displacement_next: float32 [3, 128, 32, 512], P(None, 'surf', 'rad')
- velocity_next: float32 [3, 128, 32, 512], P(None, 'surf', 'rad')
- potential: float32 [32, 8, 128], P('surf', 'rad')
The draws below stay inside these ranges and needn't reach their ends.
All inputs are finite; a program needn't handle non-finite values.
Results may differ from the reference program's by a relative error of at most 0.0003.
Values sent between devices are 32-bit elements; how exact they have to be, the bound alone decides.
A program may use at most 128 MiB of HBM per device.

```python
import math
import jax
import jax.numpy as jnp
import numpy as np
from jax import lax

EX = 4
EY = 128
SHELL = 4
CYCLES = 2
STEPS = 3
NXE = 32
NZE = 8
NXN = 128
NZN = 32
NYN = 512
N_SURF = 8


def block_levels(key, shape, cuts, low, largest):
    gain, own = 1.0, jax.random.fold_in(key, 6)
    for axis_at, shards_of in cuts:
        heights = jnp.exp(jax.random.uniform(jax.random.fold_in(own, axis_at), (shards_of,), jnp.float32, low / len(cuts), largest / len(cuts)))
        gain = gain * jnp.repeat(heights, shape[axis_at] // shards_of).reshape([-1 if axis == axis_at else 1 for axis in range(len(shape))])
    return gain


def bell_draw(stream_key, dims, scale, most, cuts=(), kind=jnp.bfloat16):
    gain = block_levels(stream_key, dims, cuts, -0.22, 0.18) if cuts else 1.0
    values = jax.random.normal(stream_key, dims, jnp.float32) * scale * gain
    return jnp.minimum(jnp.maximum(values, -most), most).astype(kind)


def setup_inputs(seed: int = 0) -> dict:
    key_of = jax.random.split(jax.random.key(seed), 8)
    return {
        "displacement": bell_draw(key_of[0], (3, NXN, NZN, NYN), 1.0, 6.0, ((1, 8), (2, 4)), jnp.float32),
        "velocity": bell_draw(key_of[1], (3, NXN, NZN, NYN), 1.0, 6.0, ((1, 8), (2, 4)), jnp.float32),
        "source": bell_draw(key_of[2], (3, NXN, NZN, NYN), 1.0, 6.0, ((1, 8), (2, 4)), jnp.float32),
        "lame_first": jnp.clip(jnp.exp(math.log(2.0) - 1.3862944 * jax.random.uniform(key_of[3], (NXN, NZN, NYN), jnp.float32) ** block_levels(key_of[3], (NXN, NZN, NYN), ((0, 8), (1, 4)), -0.2, 0.2)), 0.5, 2.0),
        "shear_modulus": jnp.clip(jnp.exp(math.log(2.0) - 1.3862944 * jax.random.uniform(key_of[4], (NXN, NZN, NYN), jnp.float32) ** block_levels(key_of[4], (NXN, NZN, NYN), ((0, 8), (1, 4)), -0.2, 0.2)), 0.5, 2.0),
        "density": jnp.clip(1.0 + 2.0 * jax.random.uniform(key_of[5], (NXN, NZN, NYN), jnp.float32) ** block_levels(key_of[5], (NXN, NZN, NYN), ((0, 8), (1, 4)), -0.2, 0.2), 1.0, 3.0),
        "shell_kappa": jnp.clip(jnp.exp(math.log(4.0) - 2.0794415 * jax.random.uniform(key_of[6], (NXE, SHELL, EY), jnp.float32) ** block_levels(key_of[6], (NXE, SHELL, EY), ((0, 8),), -0.2, 0.2)), 0.5, 4.0),
    }


time_step = 0.005
coupling = 4.0
upper_margin = 1.1
spectrum_ratio = 10.0
highest = lax.Precision.HIGHEST

def node_tables():
    points = np.array([-1.0, -np.sqrt(3.0 / 7.0), 0.0, np.sqrt(3.0 / 7.0), 1.0])
    weights = np.array([0.1, 49.0 / 90.0, 32.0 / 45.0, 49.0 / 90.0, 0.1])
    scales = np.array([np.prod([points[outer] - points[inner] for inner in range(5) if inner != outer]) for outer in range(5)])
    derivative = np.zeros((5, 5))
    for row_index in range(5):
        for col_index in range(5):
            if row_index != col_index:
                derivative[row_index, col_index] = scales[row_index] / scales[col_index] / (points[row_index] - points[col_index])
            else:
                derivative[row_index, col_index] = sum((1.0 / (points[col_index] - points[inner]) for inner in range(5) if inner != col_index))
    return (derivative, weights)

def split_nodes(values, position, elements):
    pieces = [lax.slice_in_dim(values, offset, offset + 4 * (elements - 1) + 1, 4, position) for offset in range(5)]
    return jnp.stack(pieces, axis=position)

def element_forces(nodal, lame_ext, shear_ext, dense_ext):
    derivative_table, weight_table = node_tables()
    counts = [(nodal.shape[1] - 1) // 4, (nodal.shape[2] - 1) // 4, (nodal.shape[3] - 1) // 4]
    for position, elements in zip((1, 3, 5), counts):
        nodal = split_nodes(nodal, position, elements)
    materials = []
    for values in (lame_ext, shear_ext, dense_ext):
        for position, elements in zip((0, 2, 4), counts):
            values = split_nodes(values, position, elements)
        materials.append(values)
    lame_el, shear_el, dense_el = materials
    derivative = jnp.asarray(derivative_table, jnp.float32)
    weight = jnp.asarray(weight_table, jnp.float32)
    quadrature = weight[:, None, None, None, None, None] * weight[None, None, :, None, None, None] * weight[None, None, None, None, :, None]
    gradients = [jnp.einsum('pa,iaebfcg->ipebfcg', derivative, nodal, precision=highest), jnp.einsum('pb,iaebfcg->iaepfcg', derivative, nodal, precision=highest), jnp.einsum('pc,iaebfcg->iaebfpg', derivative, nodal, precision=highest)]
    dilatation = gradients[0][0] + gradients[1][1] + gradients[2][2]
    forces = []
    for component in range(3):
        terms = []
        for other in range(3):
            stress = shear_el * (gradients[other][component] + gradients[component][other])
            if other == component:
                stress = stress + lame_el * dilatation
            terms.append(quadrature * stress)
        pulled = jnp.einsum('pa,pebfcg->aebfcg', derivative, terms[0], precision=highest)
        pulled = pulled + jnp.einsum('pb,aepfcg->aebfcg', derivative, terms[1], precision=highest)
        pulled = pulled + jnp.einsum('pc,aebfpg->aebfcg', derivative, terms[2], precision=highest)
        forces.append(-pulled)
    change = -lax.optimization_barrier(jnp.sum(quadrature * dense_el * dilatation, axis=(0, 2, 4)))
    return (jnp.stack(forces), change)

def last_element(contrib, position):
    trailing = lax.index_in_dim(contrib, 4, position, keepdims=False)
    elements = trailing.shape[position]
    return lax.slice_in_dim(trailing, elements - 1, elements, 1, position)

def fold_nodes(contrib, position, entering):
    leading = lax.slice_in_dim(contrib, 0, 4, 1, position)
    trailing = lax.index_in_dim(contrib, 4, position, keepdims=False)
    elements = trailing.shape[position]
    shifted = jnp.concatenate([entering, lax.slice_in_dim(trailing, 0, elements - 1, 1, position)], axis=position)
    merged = lax.index_in_dim(leading, 0, position, keepdims=False) + shifted
    remaining = lax.slice_in_dim(leading, 1, 4, 1, position)
    leading = jnp.concatenate([jnp.expand_dims(merged, position), remaining], axis=position)
    leading = jnp.swapaxes(leading, position, position + 1)
    return leading.reshape(leading.shape[:position] + (elements * 4,) + leading.shape[position + 2:])

def line_weights(number):
    derivative_table, weight_table = node_tables()
    base = jnp.asarray([2.0 * weight_table[0], weight_table[1], weight_table[2], weight_table[3]], jnp.float32)
    return jnp.tile(base, number // 4)

def grid_operator(nodal, added):
    zero_level = jnp.zeros_like(nodal[:, :1])
    column = jnp.concatenate([zero_level, nodal, zero_level], axis=1)
    neighbors = jnp.roll(nodal, 1, 0) + jnp.roll(nodal, -1, 0) + column[:, 2:] + column[:, :-2]
    neighbors = neighbors + jnp.roll(nodal, 1, 2) + jnp.roll(nodal, -1, 2)
    return (6.0 + added) * nodal - neighbors

def smooth(forcing, apply_operator):
    potential_all = jnp.zeros_like(forcing)
    residual = forcing
    for cycle_index in range(CYCLES):
        applied = apply_operator(residual)
        upper_bound = upper_margin * jnp.sum(applied * applied) / jnp.sum(residual * applied)
        lower_bound = upper_bound / spectrum_ratio
        midpoint = 0.5 * (upper_bound + lower_bound)
        half_width = 0.5 * (upper_bound - lower_bound)
        spread = midpoint / half_width
        previous = 1.0 / spread
        correction = residual / midpoint
        potential_all = potential_all + correction
        residual = residual - applied / midpoint
        for step_index in range(1, STEPS):
            weighting = 1.0 / (2.0 * spread - previous)
            correction = weighting * previous * correction + 2.0 * weighting / half_width * residual
            previous = weighting
            potential_all = potential_all + correction
            residual = residual - apply_operator(correction)
    return potential_all

def reference(displacement, velocity, source, lame_first, shear_modulus, density, shell_kappa):
    derivative_table, weight_table = node_tables()
    disp_ext = jnp.concatenate([displacement, displacement[:, :1]], axis=1)
    mats = [jnp.concatenate([values, values[:1]], axis=0) for values in (lame_first, shear_modulus, density)]
    disp_ext = jnp.concatenate([disp_ext, jnp.zeros_like(disp_ext[:, :, :1])], axis=2)
    mats = [jnp.concatenate([values, jnp.zeros_like(values[:, :1])], axis=1) for values in mats]
    disp_ext = jnp.concatenate([disp_ext, disp_ext[..., :1]], axis=3)
    mats = [jnp.concatenate([values, values[..., :1]], axis=2) for values in mats]

    def block_forces(block):
        start = (block * (4 * EX)).astype(jnp.int32)
        nodal = lax.dynamic_slice_in_dim(disp_ext, start, 4 * EX + 1, 1)
        pieces = [lax.dynamic_slice_in_dim(values, start, 4 * EX + 1, 0) for values in mats]
        forces, change = element_forces(nodal, pieces[0], pieces[1], pieces[2])
        forces = fold_nodes(forces, 5, last_element(forces, 5))
        forces = fold_nodes(forces, 3, jnp.zeros_like(last_element(forces, 3)))
        return (forces, change)
    blocks_out, changes = lax.map(block_forces, jnp.arange(N_SURF, dtype=jnp.int32))
    forces = jnp.moveaxis(blocks_out, 0, 2)
    forces = forces.reshape((3, 5, NXE) + forces.shape[4:])
    forces = fold_nodes(forces, 1, last_element(forces, 1))
    change = changes.reshape((NXE, NZE, EY))
    weight_x = line_weights(NXN)
    weight_z = line_weights(NZN)
    weight_z = jnp.where(jnp.arange(NZN) == 0, jnp.float32(weight_table[0]), weight_z)
    weight_y = line_weights(NYN)
    nodal_mass = density * weight_x[:, None, None] * weight_z[None, :, None] * weight_y[None, None, :]
    acceleration = (forces + source) / nodal_mass[None]
    velocity_next = velocity + time_step * acceleration
    displacement_next = displacement + time_step * velocity_next
    shell_zero = jnp.zeros((NXE, SHELL, EY), jnp.float32)
    forcing = jnp.concatenate([coupling * change, shell_zero], axis=1)
    added = jnp.concatenate([jnp.zeros_like(change), shell_kappa], axis=1)
    potential_all = smooth(forcing, lambda nodal: grid_operator(nodal, added))
    return (displacement_next, velocity_next, potential_all[:, :NZE])
```

```python
import functools

import jax
import jax.numpy as jnp
import numpy as np
from jax import lax
from jax.experimental import pallas as pl
from jax.experimental.pallas import tpu as pltpu
from jax.sharding import PartitionSpec as P

CYCLES = 2
STEPS = 3

time_step = 0.005
coupling = 4.0
upper_margin = 1.1
spectrum_ratio = 10.0
MESH = pl.DeviceIdType.MESH
VMEM = pl.BlockSpec(memory_space=pltpu.VMEM)
SMEM = pl.BlockSpec(memory_space=pltpu.SMEM)
LIMIT = 48 * 1024 * 1024


def node_tables():
    points = np.array([-1.0, -np.sqrt(3.0 / 7.0), 0.0, np.sqrt(3.0 / 7.0), 1.0])
    weights = np.array([0.1, 49.0 / 90.0, 32.0 / 45.0, 49.0 / 90.0, 0.1])
    scales = np.array(
        [
            np.prod([points[outer] - points[inner] for inner in range(5) if inner != outer])
            for outer in range(5)
        ]
    )
    derivative = np.zeros((5, 5))
    for row_index in range(5):
        for col_index in range(5):
            if row_index != col_index:
                derivative[row_index, col_index] = (
                    scales[row_index] / scales[col_index] / (points[row_index] - points[col_index])
                )
            else:
                derivative[row_index, col_index] = sum(
                    (
                        1.0 / (points[col_index] - points[inner])
                        for inner in range(5)
                        if inner != col_index
                    )
                )
    return (derivative, weights)


DERIVATIVE, WEIGHTS = node_tables()


def line_product(matrix, u):
    u0, u1, u2, u3, u4 = u
    s0, d0, s1, d1 = u0 + u4, u0 - u4, u1 + u3, u1 - u3

    def scaled(terms):
        total = None
        for factor, value in terms:
            if abs(factor) < 1e-12:
                continue
            term = value * np.float32(factor)
            total = term if total is None else total + term
        return total

    even = [
        scaled(
            [
                (0.5 * (matrix[p, 0] + matrix[p, 4]), s0),
                (0.5 * (matrix[p, 1] + matrix[p, 3]), s1),
                (matrix[p, 2], u2),
            ]
        )
        for p in range(2)
    ]
    odd = [
        scaled(
            [
                (0.5 * (matrix[p, 0] - matrix[p, 4]), d0),
                (0.5 * (matrix[p, 1] - matrix[p, 3]), d1),
            ]
        )
        for p in range(3)
    ]
    return [even[0] + odd[0], even[1] + odd[1], odd[2], odd[1] - even[1], odd[0] - even[0]]


def three_parts(values):
    high = values.astype(jnp.bfloat16)
    rest = values - high.astype(jnp.float32)
    middle = rest.astype(jnp.bfloat16)
    low = (rest - middle.astype(jnp.float32)).astype(jnp.bfloat16)
    return high, middle, low


def dot(first, second):
    return jnp.dot(first, second, preferred_element_type=jnp.float32)


def row_tables(nodes_x, nodes_z):
    own = nodes_x * nodes_z
    elem_x, elem_z = nodes_x // 4, nodes_z // 4
    tile = elem_x * elem_z
    rows = own + nodes_z + nodes_x + 8
    points = -(-25 * tile // 16) * 16
    pick = np.zeros((points, rows), np.float32)
    for a in range(5):
        for b in range(5):
            for f in range(elem_z):
                for e in range(elem_x):
                    x, z = 4 * e + a, 4 * f + b
                    if x < nodes_x and z < nodes_z:
                        row = x * nodes_z + z
                    elif z < nodes_z:
                        row = own + z
                    elif x < nodes_x:
                        row = own + nodes_z + x
                    else:
                        row = own + nodes_z + nodes_x
                    pick[(a * 5 + b) * tile + f * elem_x + e, row] = 1.0
    return pick


def lane_tables(nodes_y):
    elem_y = nodes_y // 4
    fold = np.zeros((5 * elem_y, nodes_y), np.float32)
    for c in range(5):
        for g in range(elem_y):
            fold[c * elem_y + g, (4 * g + c) % nodes_y] = 1.0
    return fold


def halo_kernel(surf, rad, disp, lame, shear, dense, plane, level, send, recv, send_sem, recv_sem):
    s, r = lax.axis_index("surf"), lax.axis_index("rad")
    nodes_x, nodes_z = disp.shape[1], disp.shape[2]
    s_low, s_high = lax.rem(s + surf - 1, surf), lax.rem(s + 1, surf)
    r_low, r_high = lax.rem(r + rad - 1, rad), lax.rem(r + 1, rad)
    barrier = pltpu.get_barrier_semaphore()
    for target in ((s_high, r), (s, r_high), (s_high, r_high)):
        pl.semaphore_signal(barrier, inc=1, device_id=target, device_id_type=MESH)
    for i in range(6):
        ref = disp.at[i] if i < 3 else (lame, shear, dense)[i - 3]
        send[i, 0:nodes_z, :] = ref[0]
        for x in range(nodes_x):
            send[i, nodes_z + x : nodes_z + x + 1, :] = ref[x, 0:1, :]
        send[i, nodes_z + nodes_x :, :] = ref[0]
    pl.semaphore_wait(barrier, 3)
    pieces = (
        (0, nodes_z, (s_low, r)),
        (nodes_z, nodes_x, (s, r_low)),
        (nodes_z + nodes_x, 8, (s_low, r_low)),
    )
    copies = []
    for k, (start, size, target) in enumerate(pieces):
        copy = pltpu.make_async_remote_copy(
            src_ref=send.at[:, pl.ds(start, size)],
            dst_ref=recv.at[:, pl.ds(start, size)],
            send_sem=send_sem.at[k],
            recv_sem=recv_sem.at[k],
            device_id=target,
            device_id_type=MESH,
        )
        copy.start()
        copies.append(copy)
    for copy in copies:
        copy.wait()
    plane[...] = recv[:, 0:nodes_z, :]
    level[...] = jnp.where(r == rad - 1, 0.0, recv[:, nodes_z:, :])


def element_kernel(
    elem_x,
    elem_z,
    disp,
    lame,
    shear,
    dense,
    kappa,
    plane,
    level,
    unfold,
    fold,
    pick,
    gather,
    weight,
    own_out,
    plane_out,
    level_out,
    payload,
    views,
    grads,
    terms,
    force,
):
    own, nodes_y = lame.shape
    elem_y = nodes_y // 4
    tile = elem_x * elem_z
    points = pick.shape[0]
    r = lax.axis_index("rad")

    def at(i, c):
        return i, slice(c * elem_y, (c + 1) * elem_y)

    for i in range(6):
        ref = disp.at[i] if i < 3 else (lame, shear, dense)[i - 3]
        extended = jnp.concatenate([ref[...], plane[i], level[i]], axis=0)
        lanes = sum(dot(part, unfold[...]) for part in three_parts(extended))
        stacked = jnp.concatenate(three_parts(lanes), axis=0)
        picked = dot(gather[...], stacked)
        views[i, :, :nodes_y] = picked
        views[i, :, nodes_y:] = pltpu.roll(picked[:, :elem_y], elem_y - 1, 1)

    def rows(a, b):
        return pl.ds(pl.multiple_of((a * 5 + b) * tile, tile), tile)

    def lanes_of(c):
        return pl.ds(c * elem_y, elem_y)

    def x_gradients(b, carry):
        for c in range(5):
            for i in range(3):
                line = [views[i, rows(a, b), lanes_of(c)] for a in range(5)]
                for a, value in enumerate(line_product(DERIVATIVE, line)):
                    grads[i, rows(a, b), lanes_of(c)] = value
        return carry

    lax.fori_loop(0, 5, x_gradients, 0)

    def z_gradients(a, carry):
        for c in range(5):
            for i in range(3):
                line = [views[i, rows(a, b), lanes_of(c)] for b in range(5)]
                for b, value in enumerate(line_product(DERIVATIVE, line)):
                    grads[3 + i, rows(a, b), lanes_of(c)] = value
        return carry

    lax.fori_loop(0, 5, z_gradients, 0)

    def stresses(a, total):
        for b in range(5):
            here = rows(a, b)
            along = [
                line_product(DERIVATIVE, [views[i, here, lanes_of(c)] for c in range(5)])
                for i in range(3)
            ]
            toward = [[], [], []]
            for c in range(5):
                scale = weight[a * 25 + b * 5 + c]
                mu = views[4, here, lanes_of(c)] * scale
                x0, x1, x2 = [grads[i, here, lanes_of(c)] for i in range(3)]
                z0, z1, z2 = [grads[3 + i, here, lanes_of(c)] for i in range(3)]
                y0, y1, y2 = [along[i][c] for i in range(3)]
                dilatation = x0 + z1 + y2
                total = total + (views[5, here, lanes_of(c)] * scale) * dilatation
                spread = (views[3, here, lanes_of(c)] * scale) * dilatation
                double = mu + mu
                terms[0, here, lanes_of(c)] = double * x0 + spread
                terms[1, here, lanes_of(c)] = mu * (x1 + z0)
                terms[2, here, lanes_of(c)] = mu * (x2 + y0)
                terms[3, here, lanes_of(c)] = double * z1 + spread
                terms[4, here, lanes_of(c)] = mu * (z2 + y1)
                toward[0].append(mu * (x2 + y0))
                toward[1].append(mu * (z2 + y1))
                toward[2].append(double * y2 + spread)
            for i in range(3):
                for c, value in enumerate(line_product(-DERIVATIVE.T, toward[i])):
                    force[i, here, lanes_of(c)] = value
        return total

    total = lax.fori_loop(0, 5, stresses, jnp.zeros((tile, elem_y), jnp.float32))
    change = -coupling * total
    for f in range(elem_z):
        payload[f] = change[f * elem_x : (f + 1) * elem_x]
    shell = jnp.zeros((elem_x, elem_y), jnp.float32)
    for k in range(kappa.shape[1]):
        level_rows = jnp.concatenate([kappa[e, k : k + 1, :] for e in range(elem_x)], axis=0)
        shell = jnp.where(r == k, level_rows, shell)
    payload[elem_z] = shell

    def z_forces(a, carry):
        for c in range(5):
            for i, term in enumerate((1, 3, 4)):
                line = [terms[term, rows(a, b), lanes_of(c)] for b in range(5)]
                for b, value in enumerate(line_product(-DERIVATIVE.T, line)):
                    force[i, rows(a, b), lanes_of(c)] += value
        return carry

    lax.fori_loop(0, 5, z_forces, 0)

    def x_forces(b, carry):
        for c in range(5):
            for i in range(3):
                line = [terms[i, rows(a, b), lanes_of(c)] for a in range(5)]
                for a, value in enumerate(line_product(-DERIVATIVE.T, line)):
                    force[i, rows(a, b), lanes_of(c)] += value
        return carry

    lax.fori_loop(0, 5, x_forces, 0)
    if points > 25 * tile:
        force[:, 25 * tile :, :] = jnp.zeros((3, points - 25 * tile, 5 * elem_y), jnp.float32)
    nodes_z = plane_out.shape[1]
    for i in range(3):
        merged = sum(dot(pick[...], part) for part in three_parts(force[i]))
        whole = sum(dot(part, fold[...]) for part in three_parts(merged))
        own_out[i] = whole[:own]
        plane_out[i] = whole[own : own + nodes_z]
        level_out[i] = whole[own + nodes_z :]


def exchange_kernel(
    surf, rad, plane, level, payload, plane_in, level_in, cells, force_send, force_recv, send_sem, recv_sem
):
    s, r = lax.axis_index("surf"), lax.axis_index("rad")
    nodes_x = level.shape[1] - 8
    peers = surf * rad
    barrier = pltpu.get_barrier_semaphore()

    def peer_of(k):
        return (lax.rem(s + k // rad, surf), lax.rem(r + lax.rem(k, rad), rad))

    def greet(k, carry):
        pl.semaphore_signal(barrier, inc=1, device_id=peer_of(k), device_id_type=MESH)
        return carry

    lax.fori_loop(1, peers, greet, 0)
    pl.semaphore_wait(barrier, peers - 1)
    s_high, r_high = lax.rem(s + 1, surf), lax.rem(r + 1, rad)
    near = level.at[:, pl.ds(0, nodes_x)], level_in.at[:, pl.ds(0, nodes_x)]
    corner = level.at[:, pl.ds(nodes_x, 8)], level_in.at[:, pl.ds(nodes_x, 8)]
    pieces = (
        (plane, plane_in, (s_high, r)),
        (*near, (s, r_high)),
        (*corner, (s_high, r_high)),
    )

    def cell_copy(k, owner):
        return pltpu.make_async_remote_copy(
            src_ref=payload,
            dst_ref=cells.at[owner, :, lax.rem(surf - k // rad, surf)],
            send_sem=send_sem.at[k],
            recv_sem=recv_sem.at[k],
            device_id=peer_of(k),
            device_id_type=MESH,
        )

    def begin(k, carry):
        cell_copy(k, r).start()
        return carry

    lax.fori_loop(1, peers, begin, 0)
    copies = []
    for k, (source, target, peer) in enumerate(pieces):
        copy = pltpu.make_async_remote_copy(
            src_ref=source,
            dst_ref=target,
            send_sem=force_send.at[k],
            recv_sem=force_recv.at[k],
            device_id=peer,
            device_id_type=MESH,
        )
        copy.start()
        copies.append(copy)
    cells[r, :, 0] = payload[...]

    def finish(k, carry):
        copy = cell_copy(k, lax.rem(r + rad - lax.rem(k, rad), rad))
        copy.wait_send()
        copy.wait_recv()
        return carry

    lax.fori_loop(1, peers, finish, 0)
    for copy in copies:
        copy.wait()


def smooth(forcing, apply_operator):
    def total(values):
        return jnp.sum(jnp.sum(values, axis=0), axis=(0, 1), keepdims=True)[None]

    potential_all = jnp.zeros_like(forcing)
    residual = forcing
    for cycle_index in range(CYCLES):
        applied = apply_operator(residual)
        upper_bound = upper_margin * total(applied * applied) / total(residual * applied)
        lower_bound = upper_bound / spectrum_ratio
        midpoint = 0.5 * (upper_bound + lower_bound)
        half_width = 0.5 * (upper_bound - lower_bound)
        spread = midpoint / half_width
        previous = 1.0 / spread
        inverse = 1.0 / midpoint
        correction = residual * inverse
        potential_all = potential_all + correction
        residual = residual - applied * inverse
        for step_index in range(1, STEPS):
            weighting = 1.0 / (2.0 * spread - previous)
            correction = (weighting * previous) * correction + (
                2.0 * weighting / half_width
            ) * residual
            previous = weighting
            potential_all = potential_all + correction
            if cycle_index < CYCLES - 1 or step_index < STEPS - 1:
                residual = residual - apply_operator(correction)
    return potential_all


def finish_kernel(
    rad,
    disp,
    velocity,
    source,
    dense,
    own_force,
    plane_in,
    level_in,
    cells,
    weight_zy,
    disp_next,
    velocity_next,
    potential,
    held,
):
    r = lax.axis_index("rad")
    nodes_z = plane_in.shape[1]
    nodes_x = dense.shape[0] // nodes_z
    elem_x, elem_z = potential.shape[:2]
    levels = rad * elem_z
    change = [cells[k // elem_z, k % elem_z] for k in range(levels)]
    shell = jnp.stack([6.0 + cells[k, elem_z] for k in range(rad)])
    forcing = jnp.stack(change + [jnp.zeros_like(change[0])] * rad)
    width, lanes = forcing.shape[1:]

    def apply_operator(values):
        gap = jnp.zeros_like(values[:1])
        neighbors = jnp.concatenate([values[1:], gap], axis=0)
        neighbors = neighbors + jnp.concatenate([gap, values[:-1]], axis=0)
        neighbors = neighbors + pltpu.roll(values, 1, 1) + pltpu.roll(values, width - 1, 1)
        neighbors = neighbors + pltpu.roll(values, 1, 2) + pltpu.roll(values, lanes - 1, 2)
        scaled = jnp.concatenate([6.0 * values[:levels], shell * values[levels:]], axis=0)
        return scaled - neighbors

    held[...] = smooth(forcing, apply_operator)[:levels]
    for f in range(elem_z):
        mine = held[r * elem_z + f]
        for e in range(elem_x):
            potential[e, f : f + 1, :] = mine[e : e + 1]

    row = lax.broadcasted_iota(jnp.int32, weight_zy.shape, 0)
    bottom = row == 0
    table = jnp.where(jnp.logical_and(bottom, r == 0), 0.5 * weight_zy[...], weight_zy[...])
    entering = jnp.logical_and(bottom, r > 0)
    base = [2.0 * WEIGHTS[0], WEIGHTS[1], WEIGHTS[2], WEIGHTS[3]]
    for x in range(nodes_x):
        here = slice(x * nodes_z, (x + 1) * nodes_z)
        gain = time_step / (dense[here] * (table * np.float32(base[x % 4])))
        for i in range(3):
            below = level_in[i, x : x + 1, :]
            if x == 0:
                below = below + level_in[i, nodes_x : nodes_x + 1, :]
            force = own_force[i, here] + jnp.where(entering, below, 0.0)
            if x == 0:
                force = force + plane_in[i]
            speed = velocity[i, here] + gain * (force + source[i, here])
            velocity_next[i, here] = speed
            disp_next[i, here] = disp[i, here] + time_step * speed


def on_device(surf, rad, displacement, velocity, source, lame_first, shear_modulus, density, shell_kappa):
    _, nodes_x, nodes_z, nodes_y = displacement.shape
    elem_x, elem_z, elem_y = nodes_x // 4, nodes_z // 4, nodes_y // 4
    own = nodes_x * nodes_z
    tile = elem_x * elem_z
    f32 = jnp.float32
    shape = jax.ShapeDtypeStruct
    pick = row_tables(nodes_x, nodes_z)
    fold = lane_tables(nodes_y)
    points, rows = pick.shape
    bf16 = functools.partial(jnp.asarray, dtype=jnp.bfloat16)
    plane, level = pl.pallas_call(
        functools.partial(halo_kernel, surf, rad),
        out_shape=[shape((6, nodes_z, nodes_y), f32), shape((6, nodes_x + 8, nodes_y), f32)],
        in_specs=[VMEM] * 4,
        out_specs=[VMEM] * 2,
        scratch_shapes=[
            pltpu.VMEM((6, nodes_z + nodes_x + 8, nodes_y), f32),
            pltpu.VMEM((6, nodes_z + nodes_x + 8, nodes_y), f32),
            pltpu.SemaphoreType.DMA((3,)),
            pltpu.SemaphoreType.DMA((3,)),
        ],
        compiler_params=pltpu.CompilerParams(
            collective_id=0, has_side_effects=True, vmem_limit_bytes=LIMIT
        ),
    )(displacement, lame_first, shear_modulus, density)

    flat = functools.partial(jnp.reshape, shape=(3, own, nodes_y))
    flat_material = functools.partial(jnp.reshape, shape=(own, nodes_y))
    weight = np.einsum("a,b,c->abc", WEIGHTS, WEIGHTS, WEIGHTS).reshape(-1).astype(np.float32)
    own_force, plane_out, level_out, payload = pl.pallas_call(
        functools.partial(element_kernel, elem_x, elem_z),
        out_shape=[
            shape((3, own, nodes_y), f32),
            shape((3, nodes_z, nodes_y), f32),
            shape((3, nodes_x + 8, nodes_y), f32),
            shape((elem_z + 1, elem_x, elem_y), f32),
        ],
        in_specs=[VMEM] * 11 + [SMEM],
        out_specs=[VMEM] * 4,
        scratch_shapes=[
            pltpu.VMEM((6, points, 5 * elem_y), f32),
            pltpu.VMEM((6, points, 5 * elem_y), f32),
            pltpu.VMEM((5, points, 5 * elem_y), f32),
            pltpu.VMEM((3, points, 5 * elem_y), f32),
        ],
        compiler_params=pltpu.CompilerParams(vmem_limit_bytes=LIMIT),
    )(
        flat(displacement),
        flat_material(lame_first),
        flat_material(shear_modulus),
        flat_material(density),
        shell_kappa,
        plane,
        level,
        bf16(fold[:nodes_y].T),
        bf16(fold),
        bf16(pick.T),
        bf16(np.concatenate([pick] * 3, axis=1)),
        jnp.asarray(weight),
    )

    peers = surf * rad
    plane_in, level_in, cells = pl.pallas_call(
        functools.partial(exchange_kernel, surf, rad),
        out_shape=[
            shape((3, nodes_z, nodes_y), f32),
            shape((3, nodes_x + 8, nodes_y), f32),
            shape((rad, elem_z + 1, surf, elem_x, elem_y), f32),
        ],
        in_specs=[VMEM] * 3,
        out_specs=[VMEM] * 3,
        scratch_shapes=[
            pltpu.SemaphoreType.DMA((3,)),
            pltpu.SemaphoreType.DMA((3,)),
            pltpu.SemaphoreType.DMA((peers,)),
            pltpu.SemaphoreType.DMA((peers,)),
        ],
        compiler_params=pltpu.CompilerParams(
            collective_id=1, has_side_effects=True, vmem_limit_bytes=LIMIT
        ),
    )(plane_out, level_out, payload)

    line = np.array([2.0 * WEIGHTS[0], WEIGHTS[1], WEIGHTS[2], WEIGHTS[3]])
    weight_zy = np.outer(np.tile(line, elem_z), np.tile(line, elem_y)).astype(np.float32)
    disp_next, velocity_next, potential = pl.pallas_call(
        functools.partial(finish_kernel, rad),
        out_shape=[
            shape((3, own, nodes_y), f32),
            shape((3, own, nodes_y), f32),
            shape((elem_x, elem_z, elem_y), f32),
        ],
        in_specs=[VMEM] * 9,
        out_specs=[VMEM] * 3,
        scratch_shapes=[pltpu.VMEM((rad * elem_z, surf * elem_x, elem_y), f32)],
        compiler_params=pltpu.CompilerParams(vmem_limit_bytes=LIMIT),
    )(
        flat(displacement),
        flat(velocity),
        flat(source),
        flat_material(density),
        own_force,
        plane_in,
        level_in,
        cells.reshape(rad, elem_z + 1, surf * elem_x, elem_y),
        jnp.asarray(weight_zy),
    )
    return (
        disp_next.reshape(displacement.shape),
        velocity_next.reshape(displacement.shape),
        potential,
    )


def solution(mesh):
    in_specs = (
        P(None, "surf", "rad", None),
        P(None, "surf", "rad", None),
        P(None, "surf", "rad", None),
        P("surf", "rad", None),
        P("surf", "rad", None),
        P("surf", "rad", None),
        P("surf", None, None),
    )
    out_specs = (P(None, "surf", "rad", None), P(None, "surf", "rad", None), P("surf", "rad", None))
    return jax.shard_map(
        functools.partial(on_device, mesh.shape["surf"], mesh.shape["rad"]),
        mesh=mesh,
        in_specs=in_specs,
        out_specs=out_specs,
        check_vma=False,
    )
```

```python
import functools

import jax
import jax.numpy as jnp
import numpy as np
from jax import lax
from jax.experimental import pallas as pl
from jax.experimental.pallas import tpu as pltpu
from jax.sharding import PartitionSpec as P

CYCLES = 2
STEPS = 3

time_step = 0.005
coupling = 4.0
upper_margin = 1.1
spectrum_ratio = 10.0
MESH = pl.DeviceIdType.MESH
VMEM = pl.BlockSpec(memory_space=pltpu.VMEM)
HBM = pl.BlockSpec(memory_space=pltpu.HBM)
LIMIT = 48 * 1024 * 1024


def node_tables():
    points = np.array([-1.0, -np.sqrt(3.0 / 7.0), 0.0, np.sqrt(3.0 / 7.0), 1.0])
    weights = np.array([0.1, 49.0 / 90.0, 32.0 / 45.0, 49.0 / 90.0, 0.1])
    scales = np.array(
        [
            np.prod([points[outer] - points[inner] for inner in range(5) if inner != outer])
            for outer in range(5)
        ]
    )
    derivative = np.zeros((5, 5))
    for row_index in range(5):
        for col_index in range(5):
            if row_index != col_index:
                derivative[row_index, col_index] = (
                    scales[row_index] / scales[col_index] / (points[row_index] - points[col_index])
                )
            else:
                derivative[row_index, col_index] = sum(
                    (
                        1.0 / (points[col_index] - points[inner])
                        for inner in range(5)
                        if inner != col_index
                    )
                )
    return (derivative, weights)


DERIVATIVE, WEIGHTS = node_tables()


def line_product(matrix, u):
    u0, u1, u2, u3, u4 = u
    s0, d0, s1, d1 = u0 + u4, u0 - u4, u1 + u3, u1 - u3

    def scaled(terms):
        total = None
        for factor, value in terms:
            if abs(factor) < 1e-12:
                continue
            term = value * np.float32(factor)
            total = term if total is None else total + term
        return total

    even = [
        scaled(
            [
                (0.5 * (matrix[p, 0] + matrix[p, 4]), s0),
                (0.5 * (matrix[p, 1] + matrix[p, 3]), s1),
                (matrix[p, 2], u2),
            ]
        )
        for p in range(2)
    ]
    odd = [
        scaled(
            [
                (0.5 * (matrix[p, 0] - matrix[p, 4]), d0),
                (0.5 * (matrix[p, 1] - matrix[p, 3]), d1),
            ]
        )
        for p in range(3)
    ]
    return [even[0] + odd[0], even[1] + odd[1], odd[2], odd[1] - even[1], odd[0] - even[0]]


def three_parts(values):
    high = values.astype(jnp.bfloat16)
    rest = values - high.astype(jnp.float32)
    middle = rest.astype(jnp.bfloat16)
    low = (rest - middle.astype(jnp.float32)).astype(jnp.bfloat16)
    return high, middle, low


def two_parts(values):
    high = values.astype(jnp.bfloat16)
    return high, (values - high.astype(jnp.float32)).astype(jnp.bfloat16)


def dot(first, second):
    return jnp.dot(first, second, preferred_element_type=jnp.float32)


def row_tables(nodes_x, nodes_z):
    own = nodes_x * nodes_z
    elem_x, elem_z = nodes_x // 4, nodes_z // 4
    tile = elem_x * elem_z
    rows = own + nodes_z + nodes_x + 8
    points = -(-25 * tile // 16) * 16
    pick = np.zeros((points, rows), np.float32)
    for a in range(5):
        for b in range(5):
            for f in range(elem_z):
                for e in range(elem_x):
                    x, z = 4 * e + a, 4 * f + b
                    if x < nodes_x and z < nodes_z:
                        row = x * nodes_z + z
                    elif z < nodes_z:
                        row = own + z
                    elif x < nodes_x:
                        row = own + nodes_z + x
                    else:
                        row = own + nodes_z + nodes_x
                    pick[(a * 5 + b) * tile + f * elem_x + e, row] = 1.0
    return pick


def lane_tables(nodes_y):
    elem_y = nodes_y // 4
    fold = np.zeros((5 * elem_y, nodes_y), np.float32)
    for c in range(5):
        for g in range(elem_y):
            fold[c * elem_y + g, (4 * g + c) % nodes_y] = 1.0
    return fold


def step_kernel(
    surf,
    rad,
    nodes_x,
    nodes_z,
    disp,
    lame,
    shear,
    dense,
    kappa_in,
    unfold_in,
    fold_in,
    pick_in,
    gather_in,
    own_out,
    plane_in,
    level_in,
    potential,
    fields,
    level_send,
    kappa,
    unfold,
    fold,
    pick,
    gather,
    lanes,
    views,
    grads,
    terms,
    force,
    merged,
    edge,
    cells,
    lattice,
    load_sem,
    halo_send,
    halo_recv,
    column_send,
    column_recv,
    line_send,
    line_recv,
    force_send,
    force_recv,
):
    s, r = lax.axis_index("surf"), lax.axis_index("rad")
    own, nodes_y = lame.shape
    elem_x, elem_z, elem_y = nodes_x // 4, nodes_z // 4, nodes_y // 4
    tile = elem_x * elem_z
    rows_all, points = pick.shape
    edge_rows = rows_all - own

    def line_peer(k):
        return lax.rem(s + k, surf), r

    def column_peer(k):
        return s, lax.rem(r + k, rad)

    low = lax.rem(s + surf - 1, surf), lax.rem(r + rad - 1, rad)
    high = lax.rem(s + 1, surf), lax.rem(r + 1, rad)
    barrier = pltpu.get_barrier_semaphore()

    def greet(target):
        pl.semaphore_signal(barrier, inc=1, device_id=target, device_id_type=MESH)

    def greet_line(k, carry):
        greet(line_peer(k))
        return carry

    loads = [(disp.at[i], fields.at[i, pl.ds(0, own)]) for i in range(3)]
    loads += [(ref, fields.at[3 + i, pl.ds(0, own)]) for i, ref in enumerate((lame, shear, dense))]
    loads += [(unfold_in, unfold), (gather_in, gather), (pick_in, pick), (fold_in, fold)]
    loads += [(kappa_in, kappa)]
    loads = [
        pltpu.make_async_copy(source, target, load_sem.at[k])
        for k, (source, target) in enumerate(loads)
    ]
    for load in loads:
        load.start()
    greet(low)
    greet(high)
    for k in range(1, rad):
        greet(column_peer(k))
    lax.fori_loop(1, surf, greet_line, 0)

    for load in loads[:6]:
        load.wait()
    for i in range(6):
        for x in range(nodes_x):
            level_send[i, x : x + 1, :] = fields[i, x * nodes_z : x * nodes_z + 1, :]
    pl.semaphore_wait(barrier, surf + rad)

    def remote(source, target, sems, k, peer):
        return pltpu.make_async_remote_copy(
            src_ref=source,
            dst_ref=target,
            send_sem=sems[0].at[k],
            recv_sem=sems[1].at[k],
            device_id=peer,
            device_id_type=MESH,
        )

    halo = (halo_send, halo_recv)
    first = fields.at[:, pl.ds(0, nodes_z)]
    halos = [
        remote(first, fields.at[:, pl.ds(own, nodes_z)], halo, 0, (low[0], r)),
        remote(level_send, fields.at[:, pl.ds(own + nodes_z, nodes_x)], halo, 1, (s, low[1])),
        remote(
            fields.at[:, pl.ds(0, 8)], fields.at[:, pl.ds(own + nodes_z + nodes_x, 8)], halo, 2, low
        ),
    ]
    for copy in halos:
        copy.start()
    for load in loads[6:]:
        load.wait()
    for i in range(6):
        split = jnp.concatenate(three_parts(fields[i, :own]), axis=0)
        spread = dot(split, unfold[...]).astype(jnp.bfloat16)
        for part in range(3):
            lanes[i, part * rows_all : part * rows_all + own] = spread[part * own : (part + 1) * own]
    for copy in halos:
        copy.wait_recv()
    split = []
    for i in range(6):
        outer = jnp.where(r == rad - 1, 0.0, fields[i, own + nodes_z :])
        split += three_parts(jnp.concatenate([fields[i, own : own + nodes_z], outer], axis=0))
    spread = dot(jnp.concatenate(split, axis=0), unfold[...]).astype(jnp.bfloat16)
    for i in range(6):
        for part in range(3):
            start = (3 * i + part) * edge_rows
            lanes[i, part * rows_all + own : (part + 1) * rows_all] = spread[
                start : start + edge_rows
            ]
    for i in range(6):
        picked = dot(gather[...], lanes[i])
        views[i, :, :nodes_y] = picked
        views[i, :, nodes_y:] = pltpu.roll(picked[:, :elem_y], elem_y - 1, 1)

    def rows(a, b):
        return pl.ds(pl.multiple_of((a * 5 + b) * tile, tile), tile)

    def lanes_of(c):
        return pl.ds(c * elem_y, elem_y)

    def x_gradients(b, carry):
        for c in range(5):
            for i in range(3):
                line = [views[i, rows(a, b), lanes_of(c)] for a in range(5)]
                for a, value in enumerate(line_product(DERIVATIVE, line)):
                    grads[i, rows(a, b), lanes_of(c)] = value
        return carry

    lax.fori_loop(0, 5, x_gradients, 0)

    def stresses(a, total):
        outer_weight = jnp.where(
            jnp.logical_or(a == 0, a == 4),
            np.float32(WEIGHTS[0]),
            jnp.where(a == 2, np.float32(WEIGHTS[2]), np.float32(WEIGHTS[1])),
        )
        outer_weight = jnp.full((tile, elem_y), outer_weight, jnp.float32)
        for c in range(5):
            for i in range(3):
                line = [views[i, rows(a, b), lanes_of(c)] for b in range(5)]
                for b, value in enumerate(line_product(DERIVATIVE, line)):
                    grads[3 + i, rows(a, b), lanes_of(c)] = value
        for b in range(5):
            here = rows(a, b)
            along = [
                line_product(DERIVATIVE, [views[i, here, lanes_of(c)] for c in range(5)])
                for i in range(3)
            ]
            toward = [[], [], []]
            for c in range(5):
                scale = outer_weight * np.float32(WEIGHTS[b] * WEIGHTS[c])
                mu = views[4, here, lanes_of(c)] * scale
                x0, x1, x2 = [grads[i, here, lanes_of(c)] for i in range(3)]
                z0, z1, z2 = [grads[3 + i, here, lanes_of(c)] for i in range(3)]
                y0, y1, y2 = [along[i][c] for i in range(3)]
                dilatation = (x0 + z1) + y2
                total = total + (views[5, here, lanes_of(c)] * scale) * dilatation
                bulk = (views[3, here, lanes_of(c)] * scale) * dilatation
                double = mu + mu
                terms[0, here, lanes_of(c)] = double * x0 + bulk
                terms[1, here, lanes_of(c)] = mu * (x1 + z0)
                terms[2, here, lanes_of(c)] = mu * (x2 + y0)
                terms[3, here, lanes_of(c)] = double * z1 + bulk
                terms[4, here, lanes_of(c)] = mu * (z2 + y1)
                toward[0].append(mu * (x2 + y0))
                toward[1].append(mu * (z2 + y1))
                toward[2].append(double * y2 + bulk)
            for i in range(3):
                for c, value in enumerate(line_product(-DERIVATIVE.T, toward[i])):
                    force[i, here, lanes_of(c)] = value
        return total

    total = lax.fori_loop(0, 5, stresses, jnp.zeros((tile, elem_y), jnp.float32))
    change = -coupling * total
    for f in range(elem_z):
        cells[r, f, 0] = change[f * elem_x : (f + 1) * elem_x]
    shell = jnp.zeros((elem_x, elem_y), jnp.float32)
    for k in range(kappa.shape[1]):
        level_rows = jnp.concatenate([kappa[e, k : k + 1, :] for e in range(elem_x)], axis=0)
        shell = jnp.where(r == k, level_rows, shell)
    cells[r, elem_z, 0] = shell

    column = (column_send, column_recv)
    line = (line_send, line_recv)

    def column_copy(k, owner):
        return remote(cells.at[r, :, 0], cells.at[owner, :, 0], column, k, column_peer(k))

    def line_copy(k):
        return remote(cells.at[:, :, 0], cells.at[:, :, surf - k], line, k, line_peer(k))

    for k in range(1, rad):
        column_copy(k, r).start()

    def z_forces(a, carry):
        for c in range(5):
            for i, term in enumerate((1, 3, 4)):
                values = [terms[term, rows(a, b), lanes_of(c)] for b in range(5)]
                for b, value in enumerate(line_product(-DERIVATIVE.T, values)):
                    force[i, rows(a, b), lanes_of(c)] += value
        return carry

    lax.fori_loop(0, 5, z_forces, 0)

    def x_forces(b, carry):
        for c in range(5):
            for i in range(3):
                values = [terms[i, rows(a, b), lanes_of(c)] for a in range(5)]
                for a, value in enumerate(line_product(-DERIVATIVE.T, values)):
                    force[i, rows(a, b), lanes_of(c)] += value
        return carry

    lax.fori_loop(0, 5, x_forces, 0)
    for k in range(1, rad):
        column_copy(k, lax.rem(r + rad - k, rad)).wait_recv()

    def begin_line(k, carry):
        line_copy(k).start()
        return carry

    lax.fori_loop(1, surf, begin_line, 0)
    if points > 25 * tile:
        force[:, 25 * tile :, :] = jnp.zeros((3, points - 25 * tile, 5 * elem_y), jnp.float32)
    for i in range(3):
        total = sum(dot(pick[...], part) for part in two_parts(force[i]))
        high_part, low_part = two_parts(total)
        merged[0, i] = high_part
        merged[1, i] = low_part
    split = [merged[part, i, own:] for part in range(2) for i in range(3)]
    whole = dot(jnp.concatenate(split, axis=0), fold[...])
    for i in range(3):
        edge[i] = (
            whole[i * edge_rows : (i + 1) * edge_rows]
            + whole[(3 + i) * edge_rows : (4 + i) * edge_rows]
        )
    sems = (force_send, force_recv)
    upper = pl.ds(nodes_z, nodes_x)
    last = pl.ds(nodes_z + nodes_x, 8)
    pushes = [
        remote(edge.at[:, pl.ds(0, nodes_z)], plane_in, sems, 0, (high[0], r)),
        remote(edge.at[:, upper], level_in.at[:, pl.ds(0, nodes_x)], sems, 1, (s, high[1])),
        remote(edge.at[:, last], level_in.at[:, pl.ds(nodes_x, 8)], sems, 2, high),
    ]
    for copy in pushes:
        copy.start()
    for i in range(3):
        whole = dot(jnp.concatenate([merged[part, i, :own] for part in range(2)], axis=0), fold[...])
        own_out[i] = whole[:own] + whole[own:]

    def finish_line(k, carry):
        copy = line_copy(k)
        copy.wait_recv()
        copy.wait_send()
        return carry

    lax.fori_loop(1, surf, finish_line, 0)
    levels = rad * elem_z
    for k in range(rad):
        for f in range(elem_z + 1):
            level = k * elem_z + f if f < elem_z else levels + k
            for block in range(surf):
                lattice[level, block * elem_x : (block + 1) * elem_x] = cells[k, f, block]
    shell = 6.0 + lattice[levels:]
    forcing = jnp.concatenate([lattice[:levels], jnp.zeros_like(shell)], axis=0)
    width, depth = forcing.shape[1:]

    def apply_operator(values):
        gap = jnp.zeros_like(values[:1])
        neighbors = jnp.concatenate([values[1:], gap], axis=0)
        neighbors = neighbors + jnp.concatenate([gap, values[:-1]], axis=0)
        neighbors = neighbors + pltpu.roll(values, 1, 1) + pltpu.roll(values, width - 1, 1)
        neighbors = neighbors + pltpu.roll(values, 1, 2) + pltpu.roll(values, depth - 1, 2)
        scaled = jnp.concatenate([6.0 * values[:levels], shell * values[levels:]], axis=0)
        return scaled - neighbors

    lattice[:levels] = smooth(forcing, apply_operator)[:levels]
    for f in range(elem_z):
        potential[f] = lattice[r * elem_z + f, :elem_x]
    for copy in halos:
        copy.wait_send()
    for k in range(1, rad):
        column_copy(k, r).wait_send()
    for copy in pushes:
        copy.wait()


def smooth(forcing, apply_operator):
    def total(values):
        return jnp.sum(jnp.sum(values, axis=0), axis=(0, 1), keepdims=True)[None]

    potential_all = jnp.zeros_like(forcing)
    residual = forcing
    for cycle_index in range(CYCLES):
        applied = apply_operator(residual)
        upper_bound = upper_margin * total(applied * applied) / total(residual * applied)
        lower_bound = upper_bound / spectrum_ratio
        midpoint = 0.5 * (upper_bound + lower_bound)
        half_width = 0.5 * (upper_bound - lower_bound)
        spread = midpoint / half_width
        previous = 1.0 / spread
        inverse = 1.0 / midpoint
        correction = residual * inverse
        potential_all = potential_all + correction
        residual = residual - applied * inverse
        for step_index in range(1, STEPS):
            weighting = 1.0 / (2.0 * spread - previous)
            correction = (weighting * previous) * correction + (
                2.0 * weighting / half_width
            ) * residual
            previous = weighting
            potential_all = potential_all + correction
            if cycle_index < CYCLES - 1 or step_index < STEPS - 1:
                residual = residual - apply_operator(correction)
    return potential_all


def finish_kernel(
    disp,
    velocity,
    source,
    dense,
    own_force,
    plane_in,
    level_in,
    solved,
    weight_zy,
    disp_next,
    velocity_next,
    potential,
):
    r = lax.axis_index("rad")
    nodes_z = plane_in.shape[1]
    nodes_x = dense.shape[0] // nodes_z
    elem_x, elem_z = potential.shape[:2]
    for f in range(elem_z):
        for e in range(elem_x):
            potential[e, f : f + 1, :] = solved[f, e : e + 1, :]

    row = lax.broadcasted_iota(jnp.int32, weight_zy.shape, 0)
    bottom = row == 0
    table = jnp.where(jnp.logical_and(bottom, r == 0), 0.5 * weight_zy[...], weight_zy[...])
    entering = jnp.logical_and(bottom, r > 0)
    base = [2.0 * WEIGHTS[0], WEIGHTS[1], WEIGHTS[2], WEIGHTS[3]]
    for x in range(nodes_x):
        here = slice(x * nodes_z, (x + 1) * nodes_z)
        gain = time_step / (dense[here] * (table * np.float32(base[x % 4])))
        for i in range(3):
            below = level_in[i, x : x + 1, :]
            if x == 0:
                below = below + level_in[i, nodes_x : nodes_x + 1, :]
            force = own_force[i, here] + jnp.where(entering, below, 0.0)
            if x == 0:
                force = force + plane_in[i]
            speed = velocity[i, here] + gain * (force + source[i, here])
            velocity_next[i, here] = speed
            disp_next[i, here] = disp[i, here] + time_step * speed


def on_device(surf, rad, displacement, velocity, source, lame_first, shear_modulus, density, shell_kappa):
    _, nodes_x, nodes_z, nodes_y = displacement.shape
    elem_x, elem_z, elem_y = nodes_x // 4, nodes_z // 4, nodes_y // 4
    own = nodes_x * nodes_z
    f32 = jnp.float32
    shape = jax.ShapeDtypeStruct
    pick = row_tables(nodes_x, nodes_z)
    fold = lane_tables(nodes_y)
    points, rows = pick.shape
    bf16 = functools.partial(jnp.asarray, dtype=jnp.bfloat16)
    flat = functools.partial(jnp.reshape, shape=(3, own, nodes_y))
    flat_material = functools.partial(jnp.reshape, shape=(own, nodes_y))
    vmem = pltpu.VMEM
    dma = pltpu.SemaphoreType.DMA
    own_force, plane_in, level_in, solved = pl.pallas_call(
        functools.partial(step_kernel, surf, rad, nodes_x, nodes_z),
        out_shape=[
            shape((3, own, nodes_y), f32),
            shape((3, nodes_z, nodes_y), f32),
            shape((3, nodes_x + 8, nodes_y), f32),
            shape((elem_z, elem_x, elem_y), f32),
        ],
        in_specs=[HBM] * 9,
        out_specs=[VMEM] * 4,
        scratch_shapes=[
            vmem((6, rows, nodes_y), f32),
            vmem((6, nodes_x, nodes_y), f32),
            vmem(shell_kappa.shape, f32),
            vmem((nodes_y, nodes_y), jnp.bfloat16),
            vmem((5 * elem_y, nodes_y), jnp.bfloat16),
            vmem((rows, points), jnp.bfloat16),
            vmem((points, 3 * rows), jnp.bfloat16),
            vmem((6, 3 * rows, nodes_y), jnp.bfloat16),
            vmem((6, points, 5 * elem_y), f32),
            vmem((6, points, 5 * elem_y), f32),
            vmem((5, points, 5 * elem_y), f32),
            vmem((3, points, 5 * elem_y), f32),
            vmem((2, 3, rows, 5 * elem_y), jnp.bfloat16),
            vmem((3, rows - own, nodes_y), f32),
            vmem((rad, elem_z + 1, surf, elem_x, elem_y), f32),
            vmem((rad * (elem_z + 1), surf * elem_x, elem_y), f32),
            dma((11,)),
            dma((3,)),
            dma((3,)),
            dma((rad,)),
            dma((rad,)),
            dma((surf,)),
            dma((surf,)),
            dma((3,)),
            dma((3,)),
        ],
        compiler_params=pltpu.CompilerParams(
            collective_id=0, has_side_effects=True, vmem_limit_bytes=LIMIT
        ),
    )(
        flat(displacement),
        flat_material(lame_first),
        flat_material(shear_modulus),
        flat_material(density),
        shell_kappa,
        bf16(fold[:nodes_y].T),
        bf16(fold),
        bf16(pick.T),
        bf16(np.concatenate([pick] * 3, axis=1)),
    )

    line = np.array([2.0 * WEIGHTS[0], WEIGHTS[1], WEIGHTS[2], WEIGHTS[3]])
    weight_zy = np.outer(np.tile(line, elem_z), np.tile(line, elem_y)).astype(np.float32)
    disp_next, velocity_next, potential = pl.pallas_call(
        finish_kernel,
        out_shape=[
            shape((3, own, nodes_y), f32),
            shape((3, own, nodes_y), f32),
            shape((elem_x, elem_z, elem_y), f32),
        ],
        in_specs=[VMEM] * 9,
        out_specs=[VMEM] * 3,
        compiler_params=pltpu.CompilerParams(vmem_limit_bytes=LIMIT),
    )(
        flat(displacement),
        flat(velocity),
        flat(source),
        flat_material(density),
        own_force,
        plane_in,
        level_in,
        solved,
        jnp.asarray(weight_zy),
    )
    return (
        disp_next.reshape(displacement.shape),
        velocity_next.reshape(displacement.shape),
        potential,
    )


def solution(mesh):
    in_specs = (
        P(None, "surf", "rad", None),
        P(None, "surf", "rad", None),
        P(None, "surf", "rad", None),
        P("surf", "rad", None),
        P("surf", "rad", None),
        P("surf", "rad", None),
        P("surf", None, None),
    )
    out_specs = (P(None, "surf", "rad", None), P(None, "surf", "rad", None), P("surf", "rad", None))
    return jax.shard_map(
        functools.partial(on_device, mesh.shape["surf"], mesh.shape["rad"]),
        mesh=mesh,
        in_specs=in_specs,
        out_specs=out_specs,
        check_vma=False,
    )
```

```python
import functools

import jax
import jax.numpy as jnp
import numpy as np
from jax import lax
from jax.experimental import pallas as pl
from jax.experimental.pallas import tpu as pltpu
from jax.sharding import PartitionSpec as P

CYCLES = 2
STEPS = 3

time_step = 0.005
coupling = 4.0
upper_margin = 1.1
spectrum_ratio = 10.0
MESH = pl.DeviceIdType.MESH
VMEM = pl.BlockSpec(memory_space=pltpu.VMEM)
HBM = pl.BlockSpec(memory_space=pltpu.HBM)
LIMIT = 48 * 1024 * 1024


def node_tables():
    points = np.array([-1.0, -np.sqrt(3.0 / 7.0), 0.0, np.sqrt(3.0 / 7.0), 1.0])
    weights = np.array([0.1, 49.0 / 90.0, 32.0 / 45.0, 49.0 / 90.0, 0.1])
    scales = np.array(
        [
            np.prod([points[outer] - points[inner] for inner in range(5) if inner != outer])
            for outer in range(5)
        ]
    )
    derivative = np.zeros((5, 5))
    for row_index in range(5):
        for col_index in range(5):
            if row_index != col_index:
                derivative[row_index, col_index] = (
                    scales[row_index] / scales[col_index] / (points[row_index] - points[col_index])
                )
            else:
                derivative[row_index, col_index] = sum(
                    (
                        1.0 / (points[col_index] - points[inner])
                        for inner in range(5)
                        if inner != col_index
                    )
                )
    return (derivative, weights)


DERIVATIVE, WEIGHTS = node_tables()


def line_product(matrix, u):
    u0, u1, u2, u3, u4 = u
    s0, d0, s1, d1 = u0 + u4, u0 - u4, u1 + u3, u1 - u3

    def scaled(terms):
        total = None
        for factor, value in terms:
            if abs(factor) < 1e-12:
                continue
            term = value * np.float32(factor)
            total = term if total is None else total + term
        return total

    even = [
        scaled(
            [
                (0.5 * (matrix[p, 0] + matrix[p, 4]), s0),
                (0.5 * (matrix[p, 1] + matrix[p, 3]), s1),
                (matrix[p, 2], u2),
            ]
        )
        for p in range(2)
    ]
    odd = [
        scaled(
            [
                (0.5 * (matrix[p, 0] - matrix[p, 4]), d0),
                (0.5 * (matrix[p, 1] - matrix[p, 3]), d1),
            ]
        )
        for p in range(3)
    ]
    return [even[0] + odd[0], even[1] + odd[1], odd[2], odd[1] - even[1], odd[0] - even[0]]


def three_parts(values):
    high = values.astype(jnp.bfloat16)
    rest = values - high.astype(jnp.float32)
    middle = rest.astype(jnp.bfloat16)
    low = (rest - middle.astype(jnp.float32)).astype(jnp.bfloat16)
    return high, middle, low


def two_parts(values):
    high = values.astype(jnp.bfloat16)
    return high, (values - high.astype(jnp.float32)).astype(jnp.bfloat16)


def dot(first, second):
    return jnp.dot(first, second, preferred_element_type=jnp.float32)


def node_row(point, nodes_x, nodes_z):
    own, elem_x, elem_z = nodes_x * nodes_z, nodes_x // 4, nodes_z // 4
    tile = elem_x * elem_z
    pair = point // tile
    inside = point - pair * tile
    a = (pair * 13) >> 6
    b = pair - 5 * a
    f = inside // elem_x
    x = 4 * (inside - f * elem_x) + a
    z = 4 * f + b
    low = jnp.where(x < nodes_x, x * nodes_z + z, own + z)
    high = own + nodes_z + jnp.where(x < nodes_x, x, nodes_x)
    row = jnp.where(z < nodes_z, low, high)
    return jnp.where(point < 25 * tile, row, -1)


def selection(hits):
    return jnp.where(hits, 1.0, 0.0).astype(jnp.bfloat16)


def iotas(rows, columns):
    return tuple(lax.broadcasted_iota(jnp.int32, (rows, columns), dim) for dim in range(2))


def unfold_table(nodes_y):
    node, place = iotas(nodes_y, nodes_y)
    elem_y = nodes_y // 4
    return selection(node == 4 * (place % elem_y) + place // elem_y)


def fold_table(nodes_y):
    elem_y = nodes_y // 4
    place, node = iotas(5 * elem_y, nodes_y)
    target = 4 * (place % elem_y) + place // elem_y
    return selection(node == jnp.where(target >= nodes_y, target - nodes_y, target))


def pick_table(nodes_x, nodes_z, points):
    row, point = iotas(nodes_x * nodes_z + nodes_x + nodes_z + 8, points)
    return selection(row == node_row(point, nodes_x, nodes_z))


def own_table(nodes_x, nodes_z, points):
    own = nodes_x * nodes_z
    point, row = iotas(points, own)
    hits = selection(row == node_row(point, nodes_x, nodes_z))
    return jnp.concatenate([hits] * 3, axis=1)


EDGE_BLOCKS = [(a, b) for a in range(5) for b in range(5) if a == 4 or b == 4]


def edge_table(nodes_x, nodes_z):
    own, edge, tile = nodes_x * nodes_z, nodes_x + nodes_z + 8, nodes_x * nodes_z // 16
    place, column = iotas(len(EDGE_BLOCKS) * tile, 3 * edge)
    block = place // tile
    pair = jnp.where(block < 4, block * 5 + 4, block + 16)
    row = node_row(pair * tile + place - block * tile, nodes_x, nodes_z) - own
    inside = column % edge
    return selection(inside == row)


def step_kernel(
    surf,
    rad,
    nodes_x,
    nodes_z,
    disp,
    lame,
    shear,
    dense,
    kappa_in,
    own_out,
    plane_in,
    level_in,
    potential,
    fields,
    level_send,
    kappa,
    unfold,
    fold,
    pick,
    gather,
    lanes,
    edge_lanes,
    views,
    grads,
    terms,
    force,
    merged,
    edge,
    cells,
    lattice,
    load_sem,
    halo_send,
    halo_recv,
    column_send,
    column_recv,
    line_send,
    line_recv,
    force_send,
    force_recv,
):
    s, r = lax.axis_index("surf"), lax.axis_index("rad")
    own, nodes_y = lame.shape
    elem_x, elem_z, elem_y = nodes_x // 4, nodes_z // 4, nodes_y // 4
    tile = elem_x * elem_z
    rows_all, points = pick.shape
    edge_rows = rows_all - own

    def line_peer(k):
        return lax.rem(s + k, surf), r

    def column_peer(k):
        return s, lax.rem(r + k, rad)

    low = lax.rem(s + surf - 1, surf), lax.rem(r + rad - 1, rad)
    high = lax.rem(s + 1, surf), lax.rem(r + 1, rad)
    barrier = pltpu.get_barrier_semaphore()

    def greet(target):
        pl.semaphore_signal(barrier, inc=1, device_id=target, device_id_type=MESH)

    def greet_line(k, carry):
        greet(line_peer(k))
        return carry

    loads = [(disp.at[i], fields.at[i, pl.ds(0, own)]) for i in range(3)]
    loads += [(ref, fields.at[3 + i, pl.ds(0, own)]) for i, ref in enumerate((lame, shear, dense))]
    loads += [(kappa_in, kappa)]
    loads = [
        pltpu.make_async_copy(source, target, load_sem.at[k])
        for k, (source, target) in enumerate(loads)
    ]
    for load in loads:
        load.start()
    greet(low)
    greet(high)
    for k in range(1, rad):
        greet(column_peer(k))
    lax.fori_loop(1, surf, greet_line, 0)
    unfold[...] = unfold_table(nodes_y)
    gather[...] = own_table(nodes_x, nodes_z, points)

    for load in loads[:6]:
        load.wait()
    for i in range(6):
        for x in range(nodes_x):
            level_send[i, x : x + 1, :] = fields[i, x * nodes_z : x * nodes_z + 1, :]
    pl.semaphore_wait(barrier, surf + rad)

    def remote(source, target, sems, k, peer):
        return pltpu.make_async_remote_copy(
            src_ref=source,
            dst_ref=target,
            send_sem=sems[0].at[k],
            recv_sem=sems[1].at[k],
            device_id=peer,
            device_id_type=MESH,
        )

    halo = (halo_send, halo_recv)
    first = fields.at[:, pl.ds(0, nodes_z)]
    halos = [
        remote(first, fields.at[:, pl.ds(own, nodes_z)], halo, 0, (low[0], r)),
        remote(level_send, fields.at[:, pl.ds(own + nodes_z, nodes_x)], halo, 1, (s, low[1])),
        remote(
            fields.at[:, pl.ds(0, 8)], fields.at[:, pl.ds(own + nodes_z + nodes_x, 8)], halo, 2, low
        ),
    ]
    for copy in halos:
        copy.start()
    for i in range(6):
        split = jnp.concatenate(three_parts(fields[i, :own]), axis=0)
        lanes[i] = dot(split, unfold[...]).astype(jnp.bfloat16)
    for i in range(6):
        views[i, :, :nodes_y] = dot(gather[...], lanes[i])
    fold[...] = fold_table(nodes_y)
    pick[...] = pick_table(nodes_x, nodes_z, points)
    edge_gather = edge_table(nodes_x, nodes_z)
    for load in loads[6:]:
        load.wait()
    for copy in halos:
        copy.wait_recv()
    split = []
    for i in range(6):
        outer = jnp.where(r == rad - 1, 0.0, fields[i, own + nodes_z :])
        split += three_parts(jnp.concatenate([fields[i, own : own + nodes_z], outer], axis=0))
    edge_lanes[...] = dot(jnp.concatenate(split, axis=0), unfold[...]).astype(jnp.bfloat16)
    for i in range(6):
        start = 3 * i * edge_rows
        added = dot(edge_gather, edge_lanes[start : start + 3 * edge_rows])
        for k, (a, b) in enumerate(EDGE_BLOCKS):
            views[i, (a * 5 + b) * tile : (a * 5 + b + 1) * tile, :nodes_y] += added[
                k * tile : (k + 1) * tile
            ]
        views[i, :, nodes_y:] = pltpu.roll(views[i, :, :elem_y], elem_y - 1, 1)

    def rows(a, b):
        return pl.ds(pl.multiple_of((a * 5 + b) * tile, tile), tile)

    def lanes_of(c):
        return pl.ds(c * elem_y, elem_y)

    def x_gradients(b, carry):
        for c in range(5):
            for i in range(3):
                line = [views[i, rows(a, b), lanes_of(c)] for a in range(5)]
                for a, value in enumerate(line_product(DERIVATIVE, line)):
                    grads[i, rows(a, b), lanes_of(c)] = value
        return carry

    lax.fori_loop(0, 5, x_gradients, 0)

    def stresses(a, total):
        outer_weight = jnp.where(
            jnp.logical_or(a == 0, a == 4),
            np.float32(WEIGHTS[0]),
            jnp.where(a == 2, np.float32(WEIGHTS[2]), np.float32(WEIGHTS[1])),
        )
        outer_weight = jnp.full((tile, elem_y), outer_weight, jnp.float32)
        for c in range(5):
            for i in range(3):
                line = [views[i, rows(a, b), lanes_of(c)] for b in range(5)]
                for b, value in enumerate(line_product(DERIVATIVE, line)):
                    grads[3 + i, rows(a, b), lanes_of(c)] = value
        for b in range(5):
            here = rows(a, b)
            along = [
                line_product(DERIVATIVE, [views[i, here, lanes_of(c)] for c in range(5)])
                for i in range(3)
            ]
            toward = [[], [], []]
            for c in range(5):
                scale = outer_weight * np.float32(WEIGHTS[b] * WEIGHTS[c])
                mu = views[4, here, lanes_of(c)] * scale
                x0, x1, x2 = [grads[i, here, lanes_of(c)] for i in range(3)]
                z0, z1, z2 = [grads[3 + i, here, lanes_of(c)] for i in range(3)]
                y0, y1, y2 = [along[i][c] for i in range(3)]
                dilatation = (x0 + z1) + y2
                total = total + (views[5, here, lanes_of(c)] * scale) * dilatation
                bulk = (views[3, here, lanes_of(c)] * scale) * dilatation
                double = mu + mu
                terms[0, here, lanes_of(c)] = double * x0 + bulk
                terms[1, here, lanes_of(c)] = mu * (x1 + z0)
                terms[2, here, lanes_of(c)] = mu * (x2 + y0)
                terms[3, here, lanes_of(c)] = double * z1 + bulk
                terms[4, here, lanes_of(c)] = mu * (z2 + y1)
                toward[0].append(mu * (x2 + y0))
                toward[1].append(mu * (z2 + y1))
                toward[2].append(double * y2 + bulk)
            for i in range(3):
                for c, value in enumerate(line_product(-DERIVATIVE.T, toward[i])):
                    force[i, here, lanes_of(c)] = value
        return total

    total = lax.fori_loop(0, 5, stresses, jnp.zeros((tile, elem_y), jnp.float32))
    change = -coupling * total
    for f in range(elem_z):
        cells[r, f, 0] = change[f * elem_x : (f + 1) * elem_x]
    shell = jnp.zeros((elem_x, elem_y), jnp.float32)
    for k in range(kappa.shape[1]):
        level_rows = jnp.concatenate([kappa[e, k : k + 1, :] for e in range(elem_x)], axis=0)
        shell = jnp.where(r == k, level_rows, shell)
    cells[r, elem_z, 0] = shell

    column = (column_send, column_recv)
    line = (line_send, line_recv)

    def column_copy(k, owner):
        return remote(cells.at[r, :, 0], cells.at[owner, :, 0], column, k, column_peer(k))

    def line_copy(k):
        return remote(cells.at[:, :, 0], cells.at[:, :, surf - k], line, k, line_peer(k))

    for k in range(1, rad):
        column_copy(k, r).start()

    def z_forces(a, carry):
        for c in range(5):
            for i, term in enumerate((1, 3, 4)):
                values = [terms[term, rows(a, b), lanes_of(c)] for b in range(5)]
                for b, value in enumerate(line_product(-DERIVATIVE.T, values)):
                    force[i, rows(a, b), lanes_of(c)] += value
        return carry

    lax.fori_loop(0, 5, z_forces, 0)

    def x_forces(b, carry):
        for c in range(5):
            for i in range(3):
                values = [terms[i, rows(a, b), lanes_of(c)] for a in range(5)]
                for a, value in enumerate(line_product(-DERIVATIVE.T, values)):
                    force[i, rows(a, b), lanes_of(c)] += value
        return carry

    lax.fori_loop(0, 5, x_forces, 0)
    for k in range(1, rad):
        column_copy(k, lax.rem(r + rad - k, rad)).wait_recv()

    def begin_line(k, carry):
        line_copy(k).start()
        return carry

    lax.fori_loop(1, surf, begin_line, 0)
    if points > 25 * tile:
        force[:, 25 * tile :, :] = jnp.zeros((3, points - 25 * tile, 5 * elem_y), jnp.float32)
    for i in range(3):
        total = sum(dot(pick[...], part) for part in two_parts(force[i]))
        high_part, low_part = two_parts(total)
        merged[0, i] = high_part
        merged[1, i] = low_part
    split = [merged[part, i, own:] for part in range(2) for i in range(3)]
    whole = dot(jnp.concatenate(split, axis=0), fold[...])
    for i in range(3):
        edge[i] = (
            whole[i * edge_rows : (i + 1) * edge_rows]
            + whole[(3 + i) * edge_rows : (4 + i) * edge_rows]
        )
    sems = (force_send, force_recv)
    upper = pl.ds(nodes_z, nodes_x)
    last = pl.ds(nodes_z + nodes_x, 8)
    pushes = [
        remote(edge.at[:, pl.ds(0, nodes_z)], plane_in, sems, 0, (high[0], r)),
        remote(edge.at[:, upper], level_in.at[:, pl.ds(0, nodes_x)], sems, 1, (s, high[1])),
        remote(edge.at[:, last], level_in.at[:, pl.ds(nodes_x, 8)], sems, 2, high),
    ]
    for copy in pushes:
        copy.start()
    for i in range(3):
        whole = dot(jnp.concatenate([merged[part, i, :own] for part in range(2)], axis=0), fold[...])
        own_out[i] = whole[:own] + whole[own:]

    def finish_line(k, carry):
        copy = line_copy(k)
        copy.wait_recv()
        copy.wait_send()
        return carry

    lax.fori_loop(1, surf, finish_line, 0)
    levels = rad * elem_z
    for k in range(rad):
        for f in range(elem_z + 1):
            level = k * elem_z + f if f < elem_z else levels + k
            for block in range(surf):
                lattice[level, block * elem_x : (block + 1) * elem_x] = cells[k, f, block]
    shell = 6.0 + lattice[levels:]
    forcing = jnp.concatenate([lattice[:levels], jnp.zeros_like(shell)], axis=0)
    width, depth = forcing.shape[1:]

    def apply_operator(values):
        gap = jnp.zeros_like(values[:1])
        neighbors = jnp.concatenate([values[1:], gap], axis=0)
        neighbors = neighbors + jnp.concatenate([gap, values[:-1]], axis=0)
        neighbors = neighbors + pltpu.roll(values, 1, 1) + pltpu.roll(values, width - 1, 1)
        neighbors = neighbors + pltpu.roll(values, 1, 2) + pltpu.roll(values, depth - 1, 2)
        scaled = jnp.concatenate([6.0 * values[:levels], shell * values[levels:]], axis=0)
        return scaled - neighbors

    lattice[:levels] = smooth(forcing, apply_operator)[:levels]
    for f in range(elem_z):
        potential[f] = lattice[r * elem_z + f, :elem_x]
    for copy in halos:
        copy.wait_send()
    for k in range(1, rad):
        column_copy(k, r).wait_send()
    for copy in pushes:
        copy.wait()


def smooth(forcing, apply_operator):
    def total(values):
        return jnp.sum(jnp.sum(values, axis=0), axis=(0, 1), keepdims=True)[None]

    potential_all = jnp.zeros_like(forcing)
    residual = forcing
    for cycle_index in range(CYCLES):
        applied = apply_operator(residual)
        upper_bound = upper_margin * total(applied * applied) / total(residual * applied)
        lower_bound = upper_bound / spectrum_ratio
        midpoint = 0.5 * (upper_bound + lower_bound)
        half_width = 0.5 * (upper_bound - lower_bound)
        spread = midpoint / half_width
        previous = 1.0 / spread
        inverse = 1.0 / midpoint
        correction = residual * inverse
        potential_all = potential_all + correction
        residual = residual - applied * inverse
        for step_index in range(1, STEPS):
            weighting = 1.0 / (2.0 * spread - previous)
            correction = (weighting * previous) * correction + (
                2.0 * weighting / half_width
            ) * residual
            previous = weighting
            potential_all = potential_all + correction
            if cycle_index < CYCLES - 1 or step_index < STEPS - 1:
                residual = residual - apply_operator(correction)
    return potential_all


def finish_kernel(
    disp,
    velocity,
    source,
    dense,
    own_force,
    plane_in,
    level_in,
    solved,
    weight_zy,
    disp_next,
    velocity_next,
    potential,
):
    r = lax.axis_index("rad")
    nodes_z = plane_in.shape[1]
    nodes_x = dense.shape[0] // nodes_z
    elem_x, elem_z = potential.shape[:2]
    for f in range(elem_z):
        for e in range(elem_x):
            potential[e, f : f + 1, :] = solved[f, e : e + 1, :]

    row = lax.broadcasted_iota(jnp.int32, weight_zy.shape, 0)
    bottom = row == 0
    table = jnp.where(jnp.logical_and(bottom, r == 0), 0.5 * weight_zy[...], weight_zy[...])
    entering = jnp.logical_and(bottom, r > 0)
    base = [2.0 * WEIGHTS[0], WEIGHTS[1], WEIGHTS[2], WEIGHTS[3]]
    for x in range(nodes_x):
        here = slice(x * nodes_z, (x + 1) * nodes_z)
        gain = time_step / (dense[here] * (table * np.float32(base[x % 4])))
        for i in range(3):
            below = level_in[i, x : x + 1, :]
            if x == 0:
                below = below + level_in[i, nodes_x : nodes_x + 1, :]
            force = own_force[i, here] + jnp.where(entering, below, 0.0)
            if x == 0:
                force = force + plane_in[i]
            speed = velocity[i, here] + gain * (force + source[i, here])
            velocity_next[i, here] = speed
            disp_next[i, here] = disp[i, here] + time_step * speed


def on_device(surf, rad, displacement, velocity, source, lame_first, shear_modulus, density, shell_kappa):
    _, nodes_x, nodes_z, nodes_y = displacement.shape
    elem_x, elem_z, elem_y = nodes_x // 4, nodes_z // 4, nodes_y // 4
    own = nodes_x * nodes_z
    f32 = jnp.float32
    shape = jax.ShapeDtypeStruct
    rows = own + nodes_z + nodes_x + 8
    points = -(-25 * elem_x * elem_z // 16) * 16
    flat = functools.partial(jnp.reshape, shape=(3, own, nodes_y))
    flat_material = functools.partial(jnp.reshape, shape=(own, nodes_y))
    vmem = pltpu.VMEM
    dma = pltpu.SemaphoreType.DMA
    own_force, plane_in, level_in, solved = pl.pallas_call(
        functools.partial(step_kernel, surf, rad, nodes_x, nodes_z),
        out_shape=[
            shape((3, own, nodes_y), f32),
            shape((3, nodes_z, nodes_y), f32),
            shape((3, nodes_x + 8, nodes_y), f32),
            shape((elem_z, elem_x, elem_y), f32),
        ],
        in_specs=[HBM] * 5,
        out_specs=[VMEM] * 4,
        scratch_shapes=[
            vmem((6, rows, nodes_y), f32),
            vmem((6, nodes_x, nodes_y), f32),
            vmem(shell_kappa.shape, f32),
            vmem((nodes_y, nodes_y), jnp.bfloat16),
            vmem((5 * elem_y, nodes_y), jnp.bfloat16),
            vmem((rows, points), jnp.bfloat16),
            vmem((points, 3 * own), jnp.bfloat16),
            vmem((6, 3 * own, nodes_y), jnp.bfloat16),
            vmem((18 * (rows - own), nodes_y), jnp.bfloat16),
            vmem((6, points, 5 * elem_y), f32),
            vmem((6, points, 5 * elem_y), f32),
            vmem((5, points, 5 * elem_y), f32),
            vmem((3, points, 5 * elem_y), f32),
            vmem((2, 3, rows, 5 * elem_y), jnp.bfloat16),
            vmem((3, rows - own, nodes_y), f32),
            vmem((rad, elem_z + 1, surf, elem_x, elem_y), f32),
            vmem((rad * (elem_z + 1), surf * elem_x, elem_y), f32),
            dma((7,)),
            dma((3,)),
            dma((3,)),
            dma((rad,)),
            dma((rad,)),
            dma((surf,)),
            dma((surf,)),
            dma((3,)),
            dma((3,)),
        ],
        compiler_params=pltpu.CompilerParams(
            collective_id=0, has_side_effects=True, vmem_limit_bytes=LIMIT
        ),
    )(
        *[
            pltpu.with_memory_space_constraint(operand, pltpu.HBM)
            for operand in (
                flat(displacement),
                flat_material(lame_first),
                flat_material(shear_modulus),
                flat_material(density),
                shell_kappa,
            )
        ]
    )

    line = np.array([2.0 * WEIGHTS[0], WEIGHTS[1], WEIGHTS[2], WEIGHTS[3]])
    weight_zy = np.outer(np.tile(line, elem_z), np.tile(line, elem_y)).astype(np.float32)
    disp_next, velocity_next, potential = pl.pallas_call(
        finish_kernel,
        out_shape=[
            shape((3, own, nodes_y), f32),
            shape((3, own, nodes_y), f32),
            shape((elem_x, elem_z, elem_y), f32),
        ],
        in_specs=[VMEM] * 9,
        out_specs=[VMEM] * 3,
        compiler_params=pltpu.CompilerParams(vmem_limit_bytes=LIMIT),
    )(
        flat(displacement),
        flat(velocity),
        flat(source),
        flat_material(density),
        own_force,
        plane_in,
        level_in,
        solved,
        jnp.asarray(weight_zy),
    )
    return (
        disp_next.reshape(displacement.shape),
        velocity_next.reshape(displacement.shape),
        potential,
    )


def solution(mesh):
    in_specs = (
        P(None, "surf", "rad", None),
        P(None, "surf", "rad", None),
        P(None, "surf", "rad", None),
        P("surf", "rad", None),
        P("surf", "rad", None),
        P("surf", "rad", None),
        P("surf", None, None),
    )
    out_specs = (P(None, "surf", "rad", None), P(None, "surf", "rad", None), P("surf", "rad", None))
    return jax.shard_map(
        functools.partial(on_device, mesh.shape["surf"], mesh.shape["rad"]),
        mesh=mesh,
        in_specs=in_specs,
        out_specs=out_specs,
        check_vma=False,
    )
```
